128 devices in a mesh: rows: 16 (over z_lo, y, core), cols: 8 (over z_hi, x).
Axes of the slice: x: 4, y: 4, z: 4 (z_hi: 2, z_lo: 2; z = z_hi * 2 + z_lo), core: 2. Of those that a mesh axis runs over, the one named last changes fastest.
Arguments:
- diffs: bfloat16 [3072, 16384], P('rows', 'cols'), may hold values from -6 to 6
- start_vectors: float32 [16384, 128], P('rows'), may hold values from -6 to 6
Outputs:
- covariance: float32 [16384, 16384], P('cols', 'rows')
- basis: float32 [16384, 128], P('rows')
The draws below stay inside these ranges and needn't reach their ends.
All inputs are finite; a program needn't handle non-finite values.
Results may differ from the reference program's by a relative error of at most 0.0003.
Values may be sent and summed in bfloat16 or wider, within the bound.
No kernel may reach another device: no remote copies, remote signals or barrier semaphores. Data moves between devices by JAX's collectives and lax.ppermute only.
A program may use at most 128 MiB of HBM per device.

```python
import math
import jax
import jax.numpy as jnp
from jax import lax

W = 16384
K = 128
ITERS = 2
M = 3072


def shard_levels(own_key, dims, cuts, least, top_value):
    def one(position, parts):
        heights = jax.random.uniform(jax.random.fold_in(jax.random.fold_in(own_key, 6), position), (parts,), jnp.float32, least / len(cuts), top_value / len(cuts))
        return jnp.repeat(jnp.exp(heights), dims[position] // parts).reshape((-1,) + (1,) * (len(dims) - position - 1))

    gain = one(*cuts[0])
    for cut in cuts[1:]:
        gain = gain * one(*cut)
    return gain


def normal_values(own_key, shape, deviation, most, cuts=(), kind=jnp.bfloat16):
    array = jax.random.normal(own_key, shape, jnp.float32) * deviation
    if len(cuts) > 0:
        array = shard_levels(own_key, shape, cuts, -0.22, 0.18) * array
    return jnp.clip(array, min=-most, max=most).astype(kind)


def setup_inputs(seed: int = 0) -> dict:
    key_list = jax.random.split(jax.random.key(seed), 3)
    diffs = normal_values(key_list[0], (M, W), 1.0, 6.0, ((0, 16), (1, 8)))
    start_vectors = normal_values(key_list[1], (W, K), 1.0, 6.0, ((0, 16),), jnp.float32)
    return dict(diffs=diffs, start_vectors=start_vectors)


def reference(diffs, start_vectors):
    count = diffs.shape[0]
    covariance = lax.dot_general(diffs.astype(jnp.float32), diffs.astype(jnp.float32), (((0,), (0,)), ((), ())), preferred_element_type=jnp.float32) / count
    basis = start_vectors
    for step in range(ITERS):
        image = jnp.dot(covariance, basis, precision=lax.Precision.HIGHEST)
        gram = jnp.dot(image.T, image, precision=lax.Precision.HIGHEST)
        lower = jnp.linalg.cholesky(gram)
        ident = jnp.eye(gram.shape[0], dtype=gram.dtype)
        inverse = jax.scipy.linalg.solve_triangular(lower, ident, lower=True)
        basis = jnp.dot(image, inverse.T, precision=lax.Precision.HIGHEST) * math.sqrt(W)
    return (covariance, basis)
```

```python
import functools
import math

import jax
import jax.numpy as jnp
from jax import lax
from jax.experimental import pallas as pl
from jax.experimental.pallas import tpu as pltpu
from jax.sharding import PartitionSpec as P

WIDTH = 16384
TOTAL = 3072
BLOCK = 2048
PIECE = 1024
CHUNK = 192
VECTORS = 128
AXES = ("rows", "cols")
HIGHEST = lax.Precision.HIGHEST
F32 = jnp.float32
BF16 = jnp.bfloat16
VMEM_LIMIT = 60 * 1024 * 1024


def number(x, y, z, k):
    return ((z % 2 * 4 + y) * 2 + k) * 8 + z // 2 * 4 + x


def move(value, where):
    pairs = []
    for x in range(4):
        for y in range(4):
            for z in range(4):
                for k in range(2):
                    tx, ty, tz, tk = where(x, y, z, k)
                    pairs.append((number(x, y, z, k), number(tx % 4, ty % 4, tz % 4, tk % 2)))
    return lax.ppermute(value, AXES, pairs)


def sib(v):
    return move(v, lambda x, y, z, k: (x, y, z, 1 - k))


def near(v):
    return move(v, lambda x, y, z, k: (x, y, z ^ 1, k))


def far(v):
    return move(v, lambda x, y, z, k: (x, y, z ^ 2, k))


def along_x(v, d):
    return move(v, lambda x, y, z, k: (x + d, y, z, k))


def along_y(v, d):
    return move(v, lambda x, y, z, k: (x, y + d, z, k))


def swap_z(z):
    return z % 2 * 2 + z // 2


def sum_cols(v):
    v = v + along_x(v, 1) + along_x(v, -1) + along_x(v, 2)
    return v + far(v)


def gather_y(v):
    return jnp.concatenate([v, along_y(v, -1), along_y(v, 2), along_y(v, 1)], 1)


def split(v):
    hi = v.astype(BF16)
    return jnp.concatenate([hi, (v - hi.astype(F32)).astype(BF16)], 0)


def terms(v):
    hi = lax.reduce_precision(v, 8, 7)
    return jnp.concatenate([hi.astype(BF16), (v - hi).astype(BF16)], 0)


def nt(v, d):
    n = v.shape[0]
    p = lax.dot_general(terms(v), d, (((1,), (1,)), ((), ())), preferred_element_type=F32)
    return p[:n] + p[n:]


def inner(v):
    return lax.dot_general(v, v, (((1,), (1,)), ((), ())), precision=HIGHEST, preferred_element_type=F32)


def factor_kernel(gram, out):
    count = VECTORS // 8
    lane = lax.broadcasted_iota(jnp.int32, (8, VECTORS), 1)
    line = lax.broadcasted_iota(jnp.int32, (8, VECTORS), 0)
    a = [gram[8 * b:8 * b + 8, :] for b in range(count)]
    e = [jnp.where(lane == line + 8 * b, 1.0, 0.0).astype(F32) for b in range(count)]
    for g in range(count):
        cols = [
            [jnp.broadcast_to(a[b][:, 8 * g + q:8 * g + q + 1], (8, VECTORS)) for b in range(g, count)]
            for q in range(8)
        ]
        top = [a[g][q:q + 1, :] for q in range(8)]
        low = [e[g][q:q + 1, :] for q in range(8)]
        inverses = []
        for q in range(8):
            pivot = cols[q][0][q:q + 1, :]
            inverse = 1.0 / pivot
            inverses.append(inverse)
            out[8 * g + q:8 * g + q + 1, :] = low[q] * lax.rsqrt(pivot)
            for p in range(q + 1, 8):
                ratio = cols[q][0][p:p + 1, :] * inverse
                top[p] = top[p] - ratio * top[q]
                low[p] = low[p] - ratio * low[q]
                cols[p] = [c - ratio * d for c, d in zip(cols[p], cols[q])]
        for q in range(8):
            top[q] = top[q] * inverses[q]
            low[q] = low[q] * inverses[q]
        for b in range(g + 1, count):
            for q in range(8):
                a[b] = a[b] - cols[q][b - g] * top[q]
                e[b] = e[b] - cols[q][b - g] * low[q]


def inverse_factor(gram):
    return pl.pallas_call(
        factor_kernel,
        out_shape=jax.ShapeDtypeStruct((VECTORS, VECTORS), F32),
        cost_estimate=pl.CostEstimate(flops=10**9, bytes_accessed=16 * 10**6, transcendentals=0),
    )(gram)


def wait_for(ref, sem):
    pltpu.make_async_copy(ref, ref, sem).wait()


TILE = 512
TILES = BLOCK // TILE
HALF = TOTAL // 2


def fetch_left(chunks, held, sems):
    for n in range(TILES):
        for i in range(16):
            pltpu.make_async_copy(
                chunks[i].at[:, pl.ds(n * TILE, TILE)], held.at[n, pl.ds(i * CHUNK, CHUNK)], sems.at[n]
            ).start()


def set_terms(z, za, zb):
    for h, v in enumerate((za, zb)):
        hi = v[...].astype(BF16)
        z[:VECTORS, h * HALF:(h + 1) * HALF] = hi
        z[VECTORS:, h * HALF:(h + 1) * HALF] = (v[...] - hi.astype(F32)).astype(BF16)


def first_kernel(za, zb, *refs):
    chunks, (out, held, z, sems) = refs[:16], refs[16:]
    fetch_left(chunks, held, sems)
    set_terms(z, za, zb)
    out[...] = jnp.zeros_like(out)
    for n in range(TILES):
        wait_for(held.at[n], sems.at[n])
        p = jnp.dot(z[...], held[n], preferred_element_type=F32)
        image = p[:VECTORS] + p[VECTORS:]
        q = lax.dot_general(
            split(image), held[n, :CHUNK], (((1,), (1,)), ((), ())), preferred_element_type=F32
        )
        out[:, :CHUNK] += q[:VECTORS] + q[VECTORS:]
        out[:, CHUNK:] += inner(image)


def second_kernel(za, zb, inverse, *refs):
    chunks, (out, held, z, sems) = refs[:16], refs[16:]
    fetch_left(chunks, held, sems)
    set_terms(z, za, zb)
    out[...] = jnp.zeros_like(out)
    for n in range(TILES):
        wait_for(held.at[n], sems.at[n])
        p = jnp.dot(z[...], held[n], preferred_element_type=F32)
        image = (p[:VECTORS] + p[VECTORS:]) * (1.0 / (TOTAL * TOTAL))
        out[...] += inner(jnp.dot(inverse[...], image, precision=HIGHEST, preferred_element_type=F32))


def on_left(kernel, width, small, chunks):
    return pl.pallas_call(
        kernel,
        out_shape=jax.ShapeDtypeStruct((VECTORS, width), F32),
        in_specs=[pl.BlockSpec(memory_space=pltpu.VMEM)] * len(small) + [pl.BlockSpec(memory_space=pl.ANY)] * 16,
        out_specs=pl.BlockSpec(memory_space=pltpu.VMEM),
        scratch_shapes=[
            pltpu.VMEM((TILES, TOTAL, TILE), BF16),
            pltpu.VMEM((2 * VECTORS, TOTAL), BF16),
            pltpu.SemaphoreType.DMA((TILES,)),
        ],
        compiler_params=pltpu.CompilerParams(vmem_limit_bytes=VMEM_LIMIT),
        cost_estimate=pl.CostEstimate(flops=2 * 256 * TOTAL * BLOCK, bytes_accessed=14 * 10**6, transcendentals=0),
    )(*small, *chunks)


def right_copies(places, blocks, held, sem):
    for i in range(8):
        for h in range(2):
            offset = pl.multiple_of(places[2 * i + h] * CHUNK, CHUNK)
            pltpu.make_async_copy(
                blocks[i].at[pl.ds(h * CHUNK, CHUNK)], held.at[pl.ds(offset, CHUNK)], sem
            ).start()


def piece_kernel(places, za, zb, inverse, *refs):
    blocks, (out, held, z, sem) = refs[:8], refs[8:]
    right_copies(places, blocks, held, sem)
    set_terms(z, za, zb)
    wait_for(held, sem)
    p = jnp.dot(z[...], held[...], preferred_element_type=F32)
    image = (p[:VECTORS] + p[VECTORS:]) * (1.0 / (TOTAL * TOTAL))
    out[...] = jnp.dot(inverse[...], image, precision=HIGHEST, preferred_element_type=F32)


def piece_image(places, za, zb, inverse, blocks):
    return pl.pallas_call(
        piece_kernel,
        out_shape=jax.ShapeDtypeStruct((VECTORS, PIECE), F32),
        in_specs=[pl.BlockSpec(memory_space=pltpu.SMEM)]
        + [pl.BlockSpec(memory_space=pltpu.VMEM)] * 3
        + [pl.BlockSpec(memory_space=pl.ANY)] * 8,
        out_specs=pl.BlockSpec(memory_space=pltpu.VMEM),
        scratch_shapes=[
            pltpu.VMEM((TOTAL, PIECE), BF16),
            pltpu.VMEM((2 * VECTORS, TOTAL), BF16),
            pltpu.SemaphoreType.DMA,
        ],
        compiler_params=pltpu.CompilerParams(vmem_limit_bytes=VMEM_LIMIT),
        cost_estimate=pl.CostEstimate(flops=2 * 256 * TOTAL * PIECE, bytes_accessed=7 * 10**6, transcendentals=0),
    )(places, za, zb, inverse, *blocks)


def final_kernel(gram, piece, out, inverse):
    factor_kernel(gram, inverse)
    out[...] = lax.dot_general(
        piece[...], inverse[...], (((0,), (1,)), ((), ())), precision=HIGHEST, preferred_element_type=F32
    ) * math.sqrt(WIDTH)


def final_basis(gram, piece):
    return pl.pallas_call(
        final_kernel,
        out_shape=jax.ShapeDtypeStruct((PIECE, VECTORS), F32),
        scratch_shapes=[pltpu.VMEM((VECTORS, VECTORS), F32)],
        cost_estimate=pl.CostEstimate(flops=10**9, bytes_accessed=16 * 10**6, transcendentals=0),
    )(gram, piece)


def left_copies(chunks, step, slot, held, sems):
    start = pl.multiple_of(step * TILE, TILE)
    for i in range(16):
        pltpu.make_async_copy(
            chunks[i].at[:, pl.ds(start, TILE)], held.at[slot, pl.ds(i * CHUNK, CHUNK)], sems.at[slot]
        ).start()


def covariance_kernel(first, count, places, *refs):
    chunks, blocks, (out, left, right, sems, sem) = refs[:16], refs[16:24], refs[-5:]
    step = pl.program_id(0)

    @pl.when(step == 0)
    def _():
        right_copies(places, blocks, right, sem)
        left_copies(chunks, first + step, 0, left, sems)
        wait_for(right, sem)

    slot = lax.rem(step, 2)
    wait_for(left.at[slot], sems.at[slot])

    @pl.when(step + 1 < count)
    def _():
        left_copies(chunks, first + step + 1, 1 - slot, left, sems)

    p = lax.dot_general(left[slot], right[...], (((0,), (0,)), ((), ())), preferred_element_type=F32)
    out[...] = p * (1.0 / TOTAL)


def covariance_tiles(first, count, places, chunks, blocks, before):
    extra = [] if before is None else [before]
    return pl.pallas_call(
        functools.partial(covariance_kernel, first, count),
        grid=(count,),
        out_shape=jax.ShapeDtypeStruct((BLOCK, PIECE), F32),
        in_specs=[pl.BlockSpec(memory_space=pltpu.SMEM)] + [pl.BlockSpec(memory_space=pl.ANY)] * (24 + len(extra)),
        out_specs=pl.BlockSpec((TILE, PIECE), lambda i: (i + first, 0)),
        scratch_shapes=[
            pltpu.VMEM((2, TOTAL, TILE), BF16),
            pltpu.VMEM((TOTAL, PIECE), BF16),
            pltpu.SemaphoreType.DMA((2,)),
            pltpu.SemaphoreType.DMA,
        ],
        input_output_aliases={25: 0} if extra else {},
        compiler_params=pltpu.CompilerParams(vmem_limit_bytes=VMEM_LIMIT),
        cost_estimate=pl.CostEstimate(
            flops=2 * TOTAL * TILE * count * PIECE, bytes_accessed=14 * 10**6, transcendentals=0
        ),
    )(places, *chunks, *blocks, *extra)


def bar(*v):
    return lax.optimization_barrier(v)


def right_places(place):
    x, y, zh, zl, k = place
    places = []
    for dzh in range(2):
        for dx in range(4):
            for h in range(2):
                dy = (x + dx - 2 * jnp.bitwise_xor(k, h) - y) % 4
                dz = jnp.bitwise_xor(jnp.bitwise_xor(zh, dzh), zl)
                places.append((h * 4 + dy) * 2 + dz)
    return jnp.stack(places).astype(jnp.int32)


def shards(diffs, start_vectors):
    rows, cols = lax.axis_index("rows"), lax.axis_index("cols")
    k, y, zl = rows % 2, rows // 2 % 4, rows // 8
    x, zh = cols % 4, cols // 4
    places = right_places((x, y, zh, zl, k))
    own = diffs

    sent = lax.dynamic_slice_in_dim(start_vectors.T, zh * 64, 64, 0)
    got = move(sent, lambda x, y, z, k: (y, x, swap_z(z), k))
    same = lax.dynamic_slice_in_dim(own, k * PIECE, PIECE, 1)
    cross = lax.dynamic_slice_in_dim(own, (1 - k) * PIECE, PIECE, 1)
    t_same = move(same, lambda x, y, z, k: (y + 2 * k, x, swap_z(z), k))
    t_cross = move(cross, lambda x, y, z, k: (y + 2 * k, x, swap_z(z), 1 - k))
    az = near(own)
    own_sib = sib(own)
    own, own_sib, az, t_same, t_cross, got = bar(own, own_sib, az, t_same, t_cross, got)

    up, down = along_y(own, -1), along_y(own, 1)
    t = jnp.concatenate([t_same, t_cross], 0)
    kept = lax.dynamic_slice_in_dim(got, k * 32, 32, 0)
    swapped = sib(lax.dynamic_slice_in_dim(got, (1 - k) * 32, 32, 0))
    start = jnp.where(k == 0, jnp.concatenate([kept, swapped], 1), jnp.concatenate([swapped, kept], 1))
    az_sib = sib(az)
    z1 = jnp.concatenate([
        jnp.concatenate([nt(start, own), nt(start, az)], 1),
        jnp.concatenate([nt(start, own_sib), nt(start, az_sib)], 1),
    ], 0)
    z1 = sum_cols(z1)
    up, down, az, t, z1 = bar(up, down, az, t, z1)

    z_up, z_down = along_y(az, -1), along_y(az, 1)
    t_up, t_down = along_x(t, -1), along_x(t, 1)
    tz = far(t)
    near_z1 = near(z1)
    near_z1 = jnp.concatenate([near_z1[:, CHUNK:], near_z1[:, :CHUNK]], 1)
    z1 = jnp.where(zl == 0, jnp.concatenate([z1, near_z1], 0), jnp.concatenate([near_z1, z1], 0))
    up, down, z_up, z_down, t_up, t_down, tz, z1 = bar(up, down, z_up, z_down, t_up, t_down, tz, z1)

    two, z_two = along_y(up, -1), along_y(z_down, 1)
    tz_up, tz_down = along_x(tz, -1), along_x(tz, 1)
    up_sib, down_sib = sib(up), sib(down)
    two, z_two, tz_up, tz_down, up_sib, down_sib, t_up, z_up, z_down, z1 = bar(
        two, z_two, tz_up, tz_down, up_sib, down_sib, t_up, z_up, z_down, z1
    )

    t_two, tz_two = along_x(t_up, -1), along_x(tz_down, 1)
    z1 = gather_y(z1)
    z1_sib = sib(z1)
    first, second = [], []
    for g in range(2):
        for core in range(2):
            a = g * 64
            first.append(jnp.where(k == core, z1[a:a + 32], z1_sib[a + 32:a + 64]))
            second.append(jnp.where(k == core, z1[a + 32:a + 64], z1_sib[a:a + 32]))
    za, zb = jnp.concatenate(first, 0), jnp.concatenate(second, 0)
    mine = [own, az, up, z_up, two, z_two, down, z_down]
    other = [own_sib, az_sib, up_sib, sib(z_up), sib(two), sib(z_two), down_sib, sib(z_down)]
    left = mine + other
    right = [t, t_up, t_two, t_down, tz, tz_up, tz_two, tz_down]

    summed = on_left(first_kernel, CHUNK + VECTORS, (za, zb), left)
    summed = sum_cols(summed)
    z2, gram1 = summed[:, :CHUNK], summed[:, CHUNK:]
    inverse1 = inverse_factor(gram1 * (1.0 / (TOTAL * TOTAL))) * math.sqrt(WIDTH)
    z2 = gather_y(jnp.concatenate([z2, near(z2)], 1))
    z2_sib = sib(z2)
    gram2 = sum_cols(on_left(second_kernel, VECTORS, (z2, z2_sib, inverse1), left))
    covariance = covariance_tiles(0, 2, places, left, right, None)
    covariance = covariance_tiles(2, 2, places, left, right, covariance)
    piece = piece_image(places, z2, z2_sib, inverse1, right)
    return (covariance, final_basis(gram2, piece))


def solution(mesh):
    return jax.shard_map(
        shards,
        mesh=mesh,
        in_specs=(P("rows", "cols"), P("rows", None)),
        out_specs=(P("cols", "rows"), P("rows", None)),
        check_vma=False,
    )
```
